32 devices in a mesh: frames: 8 (over z, x), blocks: 4 (over y, core).
Axes of the slice: x: 2, y: 2, z: 4, core: 2. Of those that a mesh axis runs over, the one named last changes fastest.
Arguments:
- frames_data: bfloat16 [28672, 2048], P('frames', 'blocks'), may hold values from -8 to 14
- traj_ids: int32 [28672], P('frames'), may hold values from 0 to 63, never falling along the last dimension, each value on 1 to 7168 neighbouring positions
Outputs:
- cov_zero: float32 [2048, 2048], P('frames', 'blocks')
- cov_lag: float32 [2048, 2048], P('frames', 'blocks')
The draws below stay inside these ranges and needn't reach their ends.
Inputs may be any that keep to these rules, and one draw needn't show every extreme that they name: `traj_ids`: ids never fall along the frames; each trajectory is a contiguous run of 1 to 7168 frames and some trajectory has exactly 7168.
All inputs are finite; a program needn't handle non-finite values.
Results may differ from the reference program's by a relative error of at most 0.0003.
Values may be sent and summed in bfloat16 or wider, within the bound.
A program may use at most 64 MiB of HBM per device.

```python
import math
import jax
import jax.numpy as jnp
import numpy as np
from jax import lax

F = 2048
LAG = 64
FRAMES = 28672
NTRAJ = 64
MAXLEN = 7168


def draw_frames_data(key, part):
    key_mean = jax.random.fold_in(key, 11)
    key_now = jax.random.fold_in(key, 12)
    offsets = jax.random.uniform(key_mean, (F,), jnp.float32, 0.5, 2.0)
    position = jnp.arange(FRAMES, dtype=jnp.float32) / max(FRAMES - 1, 1)
    rising = 0.5 + position
    fresh_noise = jnp.clip(jax.random.normal(key_now, (FRAMES + LAG, F), jnp.float32), -5.0, 5.0)
    noise_rows = fresh_noise[LAG:] + 0.7 * fresh_noise[:FRAMES]
    values = offsets[None, :] * rising[:, None] + noise_rows
    return jnp.clip(values, -8.0, 14.0).astype(jnp.bfloat16)


def profile(number_of, total, limit, slope):
    portions = [(1 << 20) // math.isqrt(rank ** slope) + 1 for rank in range(2, number_of + 1)]
    rest, counts = total - limit - (number_of - 1), [1] * (number_of - 1)
    while rest > 0:
        movable = [i for i in range(number_of - 1) if counts[i] < limit]
        mass, left = sum([portions[i] for i in movable]), rest
        for i in movable:
            addition = min(limit - counts[i], max(1, left * portions[i] // mass), rest)
            counts[i] = counts[i] + addition
            rest = rest - addition
    return np.array([limit] + counts)


def uneven(rng, amount, total, limit, lean):
    if amount == 2:
        one = jax.random.randint(rng, (), max(1, total - limit), min(limit, total - 1) + 1)
        return jnp.stack([one, total - one])
    lengths = jnp.asarray(profile(amount, total, limit, lean), jnp.int32)
    couples = (amount - 1) // 2
    source_of, taker = lengths[1:1 + 2 * couples:2], lengths[2:2 + 2 * couples:2]
    slack = jnp.minimum(source_of - 1, limit - taker)
    moved = jax.random.randint(jax.random.fold_in(rng, 1), (couples,), 0, 1 << 20) % (slack + 1)
    lengths = lengths.at[1:1 + 2 * couples:2].set(source_of - moved).at[2:2 + 2 * couples:2].set(taker + moved)
    return lengths[jax.random.permutation(jax.random.fold_in(rng, 2), amount)]


def setup_inputs(seed: int = 0) -> dict:
    splits = jax.random.split(jax.random.key(seed), 3)
    return {
        "frames_data": draw_frames_data(jax.random.fold_in(splits[2], 71), 0),
        "traj_ids": jnp.searchsorted(jnp.cumsum(uneven(splits[1], NTRAJ, FRAMES, MAXLEN, 2)), jnp.arange(FRAMES), side="right").astype(jnp.int32),
    }


def reference(frames_data, traj_ids):
    ahead = jnp.concatenate([traj_ids[LAG:] + 1, jnp.zeros((LAG,), jnp.int32)])
    valid = ahead == traj_ids + 1
    zeros = jnp.zeros_like(frames_data)
    current = jnp.where(valid[:, None], frames_data, zeros)
    later = jnp.concatenate([frames_data[LAG:], jnp.zeros((LAG, F), frames_data.dtype)], axis=0)
    count = jnp.sum(valid.astype(jnp.float32))
    mean_zero = jnp.sum(current.astype(jnp.float32), axis=0) / count
    mean_lag = jnp.sum(jnp.where(valid[:, None], later, zeros).astype(jnp.float32), axis=0) / count
    plain = lax.dot_general(current, current, (((0,), (0,)), ((), ())), preferred_element_type=jnp.float32)
    lagged = lax.dot_general(current, later, (((0,), (0,)), ((), ())), preferred_element_type=jnp.float32)
    cov_zero = plain / count - mean_zero[:, None] * mean_zero[None, :]
    cov_lag = lagged / count - mean_zero[:, None] * mean_lag[None, :]
    return cov_zero, cov_lag
```

```python
import functools

import jax
import jax.numpy as jnp
from jax import lax
from jax.experimental import pallas as pl
from jax.experimental.pallas import tpu as pltpu
from jax.sharding import PartitionSpec as P

LAG = 64
EXTRA = 8
BEHIND = 2
MESH = pl.DeviceIdType.MESH
OVER_FRAMES = (((0,), (0,)), ((), ()))


def flip(i):
    return i + 1 - 2 * lax.rem(i, 2)


def kernel(n, m, cw, x_ref, ids_ref, out_ref, xall, xo, wide, ids, marks, base, tb, rx, rz,
           load_sem, halo_send, halo_recv, gsend, psend, fsend, grecv, xsend, xrecv, zsend, zrecv):
    f = lax.axis_index("frames")
    b = lax.axis_index("blocks")
    total, own = x_ref.shape
    gw = 2 * cw
    rb = own // 2
    parts = rb // cw
    peers = m // 2 - 1
    steps = m * parts
    side = lax.rem(f, 2)
    group = lax.div(f, 2)
    mate = flip(b)
    before = lax.rem(f + n - 1, n)
    after = lax.rem(f + 1, n)

    def peer(i):
        return lax.rem(b + 2 * (i + 1), m)

    loads = []
    for j in range(parts):
        if parts == 1:
            loads.append([pltpu.make_async_copy(x_ref, xall.at[b, j], load_sem.at[2 * j])])
        else:
            loads.append([
                pltpu.make_async_copy(
                    x_ref.at[:, pl.ds(half * rb + j * cw, cw)],
                    xall.at[b, j, :, pl.ds(half * cw, cw)],
                    load_sem.at[2 * j + half],
                )
                for half in range(2)
            ])
    natural = pltpu.make_async_copy(x_ref, xo.at[pl.ds(0, total)], load_sem.at[2 * parts])
    numbers = pltpu.make_async_copy(ids_ref, ids.at[pl.ds(0, total)], load_sem.at[2 * parts + 1])
    for copies in loads:
        for copy in copies:
            copy.start()
    natural.start()
    numbers.start()

    barrier = pltpu.get_barrier_semaphore()

    def greet(to_frames, to_blocks):
        pl.semaphore_signal(barrier, inc=1, device_id=(to_frames, to_blocks), device_id_type=MESH)

    greet(before, b)
    greet(after, b)
    greet(flip(f), b)
    greet(f, mate)
    for i in range(peers):
        greet(f, peer(i))
    for i in range(1, m):
        greet(2 * lax.rem(group + i, m) + side, b)
    pl.semaphore_wait(barrier, 4 + peers + m - 1)

    halo = [
        pltpu.make_async_remote_copy(
            x_ref.at[pl.ds(0, LAG)], xo.at[pl.ds(total, LAG)], halo_send.at[0], halo_recv.at[0],
            device_id=(before, b), device_id_type=MESH),
        pltpu.make_async_remote_copy(
            ids_ref.at[pl.ds(0, LAG)], ids.at[pl.ds(total, LAG)], halo_send.at[1], halo_recv.at[1],
            device_id=(before, b), device_id_type=MESH),
    ]
    for copy in halo:
        copy.start()

    def to_peer(i, j):
        return pltpu.make_async_remote_copy(
            xall.at[b, j], xall.at[b, j], gsend.at[i, j], grecv.at[b, j],
            device_id=(f, peer(i)), device_id_type=MESH)

    def to_mate(j):
        return pltpu.make_async_remote_copy(
            xall.at[b, j], xall.at[b, j], psend.at[j], grecv.at[b, j],
            device_id=(f, mate), device_id_type=MESH)

    def onward(i, j):
        source = peer(i)
        return pltpu.make_async_remote_copy(
            xall.at[source, j], xall.at[source, j], fsend.at[i, j], grecv.at[source, j],
            device_id=(f, mate), device_id_type=MESH)

    def arrival(source, j):
        return pltpu.make_async_remote_copy(
            xall.at[source, j], xall.at[source, j], psend.at[j], grecv.at[source, j],
            device_id=(f, mate), device_id_type=MESH)

    for j in range(parts):
        for copy in loads[j]:
            copy.wait()
        for i in range(peers):
            to_peer(i, j).start()
        to_mate(j).start()

    natural.wait()
    numbers.wait()
    for copy in halo:
        copy.wait()

    tile = LAG
    last = jnp.where(f == n - 1, total - LAG, total)

    def mask_rows(t, count):
        at = pl.multiple_of(t * tile, tile)
        here = ids[pl.ds(at, tile), :]
        there = ids[pl.ds(at + LAG, tile), :]
        row = at + lax.broadcasted_iota(jnp.int32, here.shape, 0)
        mark = jnp.where((here == there) & (row < last), 1.0, 0.0)
        mark16 = mark.astype(jnp.bfloat16)
        marks[pl.ds(at, tile), :] = mark16
        for c in range(own // 128):
            lanes = slice(c * 128, (c + 1) * 128)
            wide[pl.ds(at, tile), lanes] = xo[pl.ds(at, tile), lanes] * mark16
            wide[pl.ds(at, tile), own + c * 128:own + (c + 1) * 128] = (
                xo[pl.ds(at + LAG, tile), lanes] * mark16)
        return count + jnp.sum(mark, axis=0, keepdims=True)

    count = lax.fori_loop(0, total // tile, mask_rows, jnp.zeros((1, 128), jnp.float32))
    column_sums = lax.dot_general(
        marks[...], wide[...], OVER_FRAMES, preferred_element_type=jnp.float32)[0:EXTRA]
    row_of = lax.broadcasted_iota(jnp.int32, (EXTRA, 2 * own), 0)
    base[...] = jnp.where(row_of == 0, column_sums, 0.0)
    for c in range(2 * own // 128):
        lanes = slice(c * 128, (c + 1) * 128)
        base[:, lanes] = jnp.where(row_of[:, lanes] == 2, count, base[:, lanes])

    def place(k):
        j = lax.rem(k, parts)
        near = k < 2 * parts
        later_k = jnp.maximum(k - 2 * parts, 0)
        turn = lax.div(later_k, 2)
        i = lax.div(turn, parts)
        far = lax.rem(b + 2 * (i + 1), m)
        forwarded = lax.rem(later_k, 2)
        far_block = jnp.where(forwarded == 1, flip(far), far)
        near_block = jnp.where(k < parts, b, mate)
        return (jnp.where(near, near_block, far_block),
                jnp.where(near, j, lax.rem(turn, parts)), i, forwarded)

    def pair_copy(block, j):
        return pltpu.make_async_remote_copy(
            tb.at[block, j, 1 - side], rx.at[block, j], xsend.at[block, j], xrecv.at[block, j],
            device_id=(flip(f), b), device_id_type=MESH)

    def group_copy(block, j):
        return pltpu.make_async_remote_copy(
            tb.at[block, j, side], rz.at[group, j], zsend.at[block, j], zrecv.at[group, j],
            device_id=(2 * block + side, b), device_id_type=MESH)

    def step(k, carry):
        @pl.when(k < steps)
        def _():
            block, j, i, forwarded = place(k)

            @pl.when(k >= parts)
            def _():
                arrival(block, j).wait_recv()

            @pl.when((k >= 2 * parts) & (forwarded == 0))
            def _():
                onward(i, j).start()

            depth = total // 4
            for q in range(4):
                rows = slice(q * depth, (q + 1) * depth)
                granule = xall[block, j, rows, :]
                terms = lax.dot_general(
                    granule, wide[rows, :], OVER_FRAMES, preferred_element_type=jnp.float32)
                sums = lax.dot_general(
                    marks[rows, :], granule, OVER_FRAMES,
                    preferred_element_type=jnp.float32)[0:EXTRA]
                sums = jnp.where(lax.broadcasted_iota(jnp.int32, sums.shape, 0) == 1, sums, 0.0)
                for half in range(2):
                    value = terms[half * cw:(half + 1) * cw]
                    if q == 0:
                        tb[block, j, half, 0:cw, :] = value
                        tb[block, j, half, cw:cw + EXTRA, :] = base[...]
                    else:
                        tb[block, j, half, 0:cw, :] += value
                    tb[block, j, half, cw:cw + EXTRA, 0:gw] += sums
            pair_copy(block, j).start()

        @pl.when(k >= BEHIND)
        def _():
            block, j, _i, _forwarded = place(k - BEHIND)
            pair_copy(block, j).wait_recv()
            tb[block, j, side] += rx[block, j]

            @pl.when(block != group)
            def _():
                group_copy(block, j).start()

        return carry

    lax.fori_loop(0, steps + BEHIND, step, 0)

    for j in range(parts):
        out_ref[j] = tb[group, j, side]
        for i in range(1, m):
            source = lax.rem(group + i, m)
            pltpu.make_async_remote_copy(
                rz.at[source, j], rz.at[source, j], zsend.at[source, j], zrecv.at[source, j],
                device_id=(2 * source + side, b), device_id_type=MESH).wait_recv()
            out_ref[j] += rz[source, j]

    for j in range(parts):
        to_mate(j).wait_send()
        for i in range(peers):
            to_peer(i, j).wait_send()
            onward(i, j).wait_send()
        for i in range(m):
            pair_copy(i, j).wait_send()
        for i in range(1, m):
            group_copy(lax.rem(group + i, m), j).wait_send()


def shards(n, m, frames_data, traj_ids):
    total, own = frames_data.shape
    rb = own * m // n
    assert n == 2 * m and own == 2 * rb
    cw = min(128, rb)
    parts = rb // cw
    ids = jnp.broadcast_to(traj_ids[:, None], (total, 128))
    piece = (cw + EXTRA, 2 * own)
    sem = pltpu.SemaphoreType.DMA
    peers = m // 2 - 1
    reduced = pl.pallas_call(
        functools.partial(kernel, n, m, cw),
        out_shape=jax.ShapeDtypeStruct((parts, *piece), jnp.float32),
        in_specs=[pl.BlockSpec(memory_space=pl.ANY)] * 2,
        out_specs=pl.BlockSpec(memory_space=pltpu.VMEM),
        scratch_shapes=[
            pltpu.VMEM((m, parts, total, 2 * cw), jnp.bfloat16),
            pltpu.VMEM((total + LAG, own), jnp.bfloat16),
            pltpu.VMEM((total, 2 * own), jnp.bfloat16),
            pltpu.VMEM((total + LAG, 128), jnp.int32),
            pltpu.VMEM((total, 128), jnp.bfloat16),
            pltpu.VMEM((EXTRA, 2 * own), jnp.float32),
            pltpu.VMEM((m, parts, 2, *piece), jnp.float32),
            pltpu.VMEM((m, parts, *piece), jnp.float32),
            pltpu.VMEM((m, parts, *piece), jnp.float32),
            sem((2 * parts + 2,)),
            sem((2,)),
            sem((2,)),
            sem((peers, parts)),
            sem((parts,)),
            sem((peers, parts)),
            sem((m, parts)),
            sem((m, parts)),
            sem((m, parts)),
            sem((m, parts)),
            sem((m, parts)),
        ],
        compiler_params=pltpu.CompilerParams(
            collective_id=0, has_side_effects=True, vmem_limit_bytes=58 * 2**20),
        cost_estimate=pl.CostEstimate(
            flops=4 * total * own * own * m, bytes_accessed=4 * total * own, transcendentals=0),
    )(frames_data, ids)
    side = lax.axis_index("frames") % 2
    count = reduced[0, cw + 2, 0]
    terms = reduced[:, :cw].reshape(rb, 2 * own)
    column_means = reduced[0, cw] / count
    row_sums = lax.dynamic_slice_in_dim(reduced[:, cw + 1], side * cw, cw, 1).reshape(rb)
    cov = terms / count - (row_sums / count)[:, None] * column_means[None, :]
    return cov[:, :own], cov[:, own:]


def solution(mesh):
    n, m = mesh.shape["frames"], mesh.shape["blocks"]
    return jax.shard_map(
        functools.partial(shards, n, m),
        mesh=mesh,
        in_specs=(P("frames", "blocks"), P("frames")),
        out_specs=(P("frames", "blocks"), P("frames", "blocks")),
        check_vma=False,
    )
```

```python
import functools

import jax
import jax.numpy as jnp
from jax import lax
from jax.experimental import pallas as pl
from jax.experimental.pallas import tpu as pltpu
from jax.sharding import PartitionSpec as P

LAG = 64
EXTRA = 8
MESH = pl.DeviceIdType.MESH
OVER_FRAMES = (((0,), (0,)), ((), ()))


def flip(i):
    return i + 1 - 2 * lax.rem(i, 2)


def kernel(n, m, cw, x_ref, ids_ref, out_ref, xall, xo, wide, ids, marks, base, tb, rx, rz,
           load_sem, halo_send, halo_recv, hsend, psend, fsend, mrecv, hrecv, xsend, xrecv, zsend, zrecv):
    f = lax.axis_index("frames")
    b = lax.axis_index("blocks")
    total, own = x_ref.shape
    gw = 2 * cw
    rb = own // 2
    parts = rb // cw
    peers = m // 2 - 1
    steps = m * parts
    side = lax.rem(f, 2)
    group = lax.div(f, 2)
    levels = m.bit_length() - 1
    core = lax.rem(b, 2)
    chip = lax.div(b, 2)
    span = total // 2
    mate = flip(b)
    before = lax.rem(f + n - 1, n)
    after = lax.rem(f + 1, n)

    def peer(i):
        return lax.rem(b + 2 * (i + 1), m)

    def bit(i, p):
        return lax.rem(lax.div(i, 2**p), 2)

    def across(p):
        return group + 2**p - 2 ** (p + 1) * bit(group, p)

    loads = []
    for j in range(parts):
        if parts == 1:
            loads.append([pltpu.make_async_copy(x_ref, xall.at[b, j], load_sem.at[2 * j])])
        else:
            loads.append([
                pltpu.make_async_copy(
                    x_ref.at[:, pl.ds(half * rb + j * cw, cw)],
                    xall.at[b, j, :, pl.ds(half * cw, cw)],
                    load_sem.at[2 * j + half],
                )
                for half in range(2)
            ])
    natural = pltpu.make_async_copy(x_ref, xo.at[pl.ds(0, total)], load_sem.at[2 * parts])
    numbers = pltpu.make_async_copy(ids_ref, ids.at[pl.ds(0, total)], load_sem.at[2 * parts + 1])
    for copies in loads:
        for copy in copies:
            copy.start()
    natural.start()
    numbers.start()

    barrier = pltpu.get_barrier_semaphore()

    def greet(to_frames, to_blocks):
        pl.semaphore_signal(barrier, inc=1, device_id=(to_frames, to_blocks), device_id_type=MESH)

    greet(before, b)
    greet(after, b)
    greet(flip(f), b)
    greet(f, mate)
    for i in range(peers):
        greet(f, peer(i))
    for p in range(levels):
        greet(2 * across(p) + side, b)
    pl.semaphore_wait(barrier, 4 + peers + levels)

    halo = [
        pltpu.make_async_remote_copy(
            x_ref.at[pl.ds(0, LAG)], xo.at[pl.ds(total, LAG)], halo_send.at[0], halo_recv.at[0],
            device_id=(before, b), device_id_type=MESH),
        pltpu.make_async_remote_copy(
            ids_ref.at[pl.ds(0, LAG)], ids.at[pl.ds(total, LAG)], halo_send.at[1], halo_recv.at[1],
            device_id=(before, b), device_id_type=MESH),
    ]
    for copy in halo:
        copy.start()

    def part(block, j, which):
        return xall.at[block, j, pl.ds(pl.multiple_of(which * span, 16), span)]

    def to_peer(i, j, e):
        block = 2 * chip + e
        return pltpu.make_async_remote_copy(
            part(block, j, core), part(block, j, core), hsend.at[i, j, e], hrecv.at[block, j, core],
            device_id=(f, peer(i)), device_id_type=MESH)

    def to_mate(j):
        return pltpu.make_async_remote_copy(
            xall.at[b, j], xall.at[b, j], psend.at[j], mrecv.at[j],
            device_id=(f, mate), device_id_type=MESH)

    def from_mate(j):
        return pltpu.make_async_remote_copy(
            xall.at[mate, j], xall.at[mate, j], psend.at[j], mrecv.at[j],
            device_id=(f, mate), device_id_type=MESH)

    def onward(block, j):
        return pltpu.make_async_remote_copy(
            part(block, j, core), part(block, j, core), fsend.at[block, j], hrecv.at[block, j, core],
            device_id=(f, mate), device_id_type=MESH)

    def arrival(block, j, which):
        return pltpu.make_async_remote_copy(
            part(block, j, which), part(block, j, which), fsend.at[block, j],
            hrecv.at[block, j, which], device_id=(f, mate), device_id_type=MESH)

    for j in range(parts):
        for copy in loads[j]:
            copy.wait()
        to_mate(j).start()

    def spread(j):
        for e in range(2):
            @pl.when(core != e)
            def _():
                from_mate(j).wait_recv()

            for i in range(peers):
                to_peer(i, j, e).start()

    spread(0)
    natural.wait()
    numbers.wait()
    for copy in halo:
        copy.wait()

    tile = LAG
    last = jnp.where(f == n - 1, total - LAG, total)

    def mask_rows(t, count):
        at = pl.multiple_of(t * tile, tile)
        here = ids[pl.ds(at, tile), :]
        there = ids[pl.ds(at + LAG, tile), :]
        row = at + lax.broadcasted_iota(jnp.int32, here.shape, 0)
        mark = jnp.where((here == there) & (row < last), 1.0, 0.0)
        mark16 = mark.astype(jnp.bfloat16)
        marks[pl.ds(at, tile), :] = mark16
        for c in range(own // 128):
            lanes = slice(c * 128, (c + 1) * 128)
            wide[pl.ds(at, tile), lanes] = xo[pl.ds(at, tile), lanes] * mark16
            wide[pl.ds(at, tile), own + c * 128:own + (c + 1) * 128] = (
                xo[pl.ds(at + LAG, tile), lanes] * mark16)
        return count + jnp.sum(mark, axis=0, keepdims=True)

    count = lax.fori_loop(0, total // tile, mask_rows, jnp.zeros((1, 128), jnp.float32))
    column_sums = lax.dot_general(
        marks[...], wide[...], OVER_FRAMES, preferred_element_type=jnp.float32)[0:EXTRA]
    row_of = lax.broadcasted_iota(jnp.int32, (EXTRA, 2 * own), 0)
    base[...] = jnp.where(row_of == 0, column_sums, 0.0)
    for c in range(2 * own // 128):
        lanes = slice(c * 128, (c + 1) * 128)
        base[:, lanes] = jnp.where(row_of[:, lanes] == 2, count, base[:, lanes])

    for j in range(1, parts):
        spread(j)

    def place(k):
        j = lax.rem(k, parts)
        near = k < 2 * parts
        later_k = jnp.maximum(k - 2 * parts, 0)
        turn = lax.div(later_k, 2)
        far = lax.rem(chip + lax.div(turn, parts) + 1, m // 2)
        far_block = 2 * far + lax.rem(later_k, 2)
        near_block = jnp.where(k < parts, b, mate)
        return jnp.where(near, near_block, far_block), jnp.where(near, j, lax.rem(turn, parts))

    def pair_copy(block, j):
        return pltpu.make_async_remote_copy(
            tb.at[block, j, 1 - side], rx.at[block, j], xsend.at[block, j], xrecv.at[block, j],
            device_id=(flip(f), b), device_id_type=MESH)

    def group_copy(block, j, p):
        return pltpu.make_async_remote_copy(
            tb.at[block, j, side], rz.at[block, j, p], zsend.at[block, j], zrecv.at[block, j, p],
            device_id=(2 * across(p) + side, b), device_id_type=MESH)

    def stage(p, q, carry):
        block, j = place(q)

        @pl.when(lax.rem(group, 2**p) == lax.rem(block, 2**p))
        def _():
            if p == 0:
                pair_copy(block, j).wait_recv()
                tb[block, j, side] += rx[block, j]
            else:
                group_copy(block, j, p - 1).wait_recv()
                tb[block, j, side] += rz[block, j, p - 1]
            if p < levels:
                @pl.when(bit(group, p) != bit(block, p))
                def _():
                    group_copy(block, j, p).start()

        return carry

    def finished(p, k):
        usual = jnp.maximum(k - 1 - p, 0)
        eager = jnp.where(k == steps - 1, jnp.maximum(steps - 1 - p, 0), usual)
        return jnp.where(k < 0, 0, jnp.where(k >= steps, steps, eager))

    def step(k, carry):
        for p in range(levels + 1):
            lax.fori_loop(finished(p, k - 1), finished(p, k), functools.partial(stage, p), 0)

        @pl.when(k < steps)
        def _():
            block, j = place(k)

            @pl.when(k >= 2 * parts)
            def _():
                arrival(block, j, core).wait_recv()
                onward(block, j).start()
                arrival(block, j, 1 - core).wait_recv()

            depth = total // 4
            for q in range(4):
                rows = slice(q * depth, (q + 1) * depth)
                granule = xall[block, j, rows, :]
                terms = lax.dot_general(
                    granule, wide[rows, :], OVER_FRAMES, preferred_element_type=jnp.float32)
                sums = lax.dot_general(
                    marks[rows, :], granule, OVER_FRAMES,
                    preferred_element_type=jnp.float32)[0:EXTRA]
                sums = jnp.where(lax.broadcasted_iota(jnp.int32, sums.shape, 0) == 1, sums, 0.0)
                for half in range(2):
                    value = terms[half * cw:(half + 1) * cw]
                    if q == 0:
                        tb[block, j, half, 0:cw, :] = value
                        tb[block, j, half, cw:cw + EXTRA, :] = base[...]
                    else:
                        tb[block, j, half, 0:cw, :] += value
                    tb[block, j, half, cw:cw + EXTRA, 0:gw] += sums
            pair_copy(block, j).start()

        return carry

    lax.fori_loop(0, steps, step, 0)
    for p in range(levels + 1):
        lax.fori_loop(finished(p, steps - 1), steps, functools.partial(stage, p), 0)
    for j in range(parts):
        out_ref[j] = tb[group, j, side]

    for j in range(parts):
        to_mate(j).wait_send()
        for i in range(peers):
            for e in range(2):
                to_peer(i, j, e).wait_send()
                onward(2 * lax.rem(chip + i + 1, m // 2) + e, j).wait_send()
        for i in range(m):
            pair_copy(i, j).wait_send()
        for i in range(1, m):
            group_copy(lax.rem(group + i, m), j, 0).wait_send()


def shards(n, m, frames_data, traj_ids):
    total, own = frames_data.shape
    rb = own * m // n
    levels = m.bit_length() - 1
    assert n == 2 * m and own == 2 * rb and m == 2**levels
    cw = min(128, rb)
    parts = rb // cw
    ids = jnp.broadcast_to(traj_ids[:, None], (total, 128))
    piece = (cw + EXTRA, 2 * own)
    sem = pltpu.SemaphoreType.DMA
    peers = m // 2 - 1
    reduced = pl.pallas_call(
        functools.partial(kernel, n, m, cw),
        out_shape=jax.ShapeDtypeStruct((parts, *piece), jnp.float32),
        in_specs=[pl.BlockSpec(memory_space=pl.ANY)] * 2,
        out_specs=pl.BlockSpec(memory_space=pltpu.VMEM),
        scratch_shapes=[
            pltpu.VMEM((m, parts, total, 2 * cw), jnp.bfloat16),
            pltpu.VMEM((total + LAG, own), jnp.bfloat16),
            pltpu.VMEM((total, 2 * own), jnp.bfloat16),
            pltpu.VMEM((total + LAG, 128), jnp.int32),
            pltpu.VMEM((total, 128), jnp.bfloat16),
            pltpu.VMEM((EXTRA, 2 * own), jnp.float32),
            pltpu.VMEM((m, parts, 2, *piece), jnp.float32),
            pltpu.VMEM((m, parts, *piece), jnp.float32),
            pltpu.VMEM((m, parts, levels, *piece), jnp.float32),
            sem((2 * parts + 2,)),
            sem((2,)),
            sem((2,)),
            sem((peers, parts, 2)),
            sem((parts,)),
            sem((m, parts)),
            sem((parts,)),
            sem((m, parts, 2)),
            sem((m, parts)),
            sem((m, parts)),
            sem((m, parts)),
            sem((m, parts, levels)),
        ],
        compiler_params=pltpu.CompilerParams(
            collective_id=0, has_side_effects=True, vmem_limit_bytes=58 * 2**20),
        cost_estimate=pl.CostEstimate(
            flops=4 * total * own * own * m, bytes_accessed=4 * total * own, transcendentals=0),
    )(frames_data, ids)
    side = lax.axis_index("frames") % 2
    count = reduced[0, cw + 2, 0]
    terms = reduced[:, :cw].reshape(rb, 2 * own)
    column_means = reduced[0, cw] / count
    row_sums = lax.dynamic_slice_in_dim(reduced[:, cw + 1], side * cw, cw, 1).reshape(rb)
    cov = terms / count - (row_sums / count)[:, None] * column_means[None, :]
    return cov[:, :own], cov[:, own:]


def solution(mesh):
    n, m = mesh.shape["frames"], mesh.shape["blocks"]
    return jax.shard_map(
        functools.partial(shards, n, m),
        mesh=mesh,
        in_specs=(P("frames", "blocks"), P("frames")),
        out_specs=(P("frames", "blocks"), P("frames", "blocks")),
        check_vma=False,
    )
```

```python
import functools

import jax
import jax.numpy as jnp
from jax import lax
from jax.experimental import pallas as pl
from jax.experimental.pallas import tpu as pltpu
from jax.sharding import PartitionSpec as P

LAG = 64
EXTRA = 8
MESH = pl.DeviceIdType.MESH
OVER_FRAMES = (((0,), (0,)), ((), ()))


def flip(i):
    return i + 1 - 2 * lax.rem(i, 2)


def kernel(n, m, cw, x_ref, ids_ref, out_ref, xall, xo, wide, ids, marks, base, tb, rx, rz,
           load_sem, halo_send, halo_recv, hsend, psend, fsend, mrecv, hrecv, xsend, xrecv, zsend, zrecv):
    f = lax.axis_index("frames")
    b = lax.axis_index("blocks")
    total, own = x_ref.shape
    gw = 2 * cw
    rb = own // 2
    parts = rb // cw
    peers = m // 2 - 1
    steps = m * parts
    side = lax.rem(f, 2)
    group = lax.div(f, 2)
    levels = m.bit_length() - 1
    core = lax.rem(b, 2)
    chip = lax.div(b, 2)
    span = total // 2
    mate = flip(b)
    before = lax.rem(f + n - 1, n)
    after = lax.rem(f + 1, n)

    def peer(i):
        return lax.rem(b + 2 * (i + 1), m)

    def bit(i, p):
        return lax.rem(lax.div(i, 2**p), 2)

    def across(p):
        return group + 2**p - 2 ** (p + 1) * bit(group, p)

    loads = []
    for j in range(parts):
        if parts == 1:
            loads.append([pltpu.make_async_copy(x_ref, xall.at[b, j], load_sem.at[2 * j])])
        else:
            loads.append([
                pltpu.make_async_copy(
                    x_ref.at[:, pl.ds(half * rb + j * cw, cw)],
                    xall.at[b, j, :, pl.ds(half * cw, cw)],
                    load_sem.at[2 * j + half],
                )
                for half in range(2)
            ])
    natural = pltpu.make_async_copy(x_ref, xo.at[pl.ds(0, total)], load_sem.at[2 * parts])
    numbers = pltpu.make_async_copy(ids_ref, ids.at[pl.ds(0, total)], load_sem.at[2 * parts + 1])
    for copies in loads:
        for copy in copies:
            copy.start()
    natural.start()
    numbers.start()

    barrier = pltpu.get_barrier_semaphore()

    def greet(to_frames, to_blocks):
        pl.semaphore_signal(barrier, inc=1, device_id=(to_frames, to_blocks), device_id_type=MESH)

    greet(before, b)
    greet(after, b)
    greet(flip(f), b)
    greet(f, mate)
    for i in range(peers):
        greet(f, peer(i))
    for p in range(levels):
        greet(2 * across(p) + side, b)
    pl.semaphore_wait(barrier, 4 + peers + levels)

    halo = [
        pltpu.make_async_remote_copy(
            x_ref.at[pl.ds(0, LAG)], xo.at[pl.ds(total, LAG)], halo_send.at[0], halo_recv.at[0],
            device_id=(before, b), device_id_type=MESH),
        pltpu.make_async_remote_copy(
            ids_ref.at[pl.ds(0, LAG)], ids.at[pl.ds(total, LAG)], halo_send.at[1], halo_recv.at[1],
            device_id=(before, b), device_id_type=MESH),
    ]
    for copy in halo:
        copy.start()

    def part(block, j, which):
        return xall.at[block, j, pl.ds(pl.multiple_of(which * span, 16), span)]

    def to_peer(i, j, e):
        block = 2 * chip + e
        return pltpu.make_async_remote_copy(
            part(block, j, core), part(block, j, core), hsend.at[i, j, e], hrecv.at[block, j, core],
            device_id=(f, peer(i)), device_id_type=MESH)

    def to_mate(j):
        return pltpu.make_async_remote_copy(
            xall.at[b, j], xall.at[b, j], psend.at[j], mrecv.at[j],
            device_id=(f, mate), device_id_type=MESH)

    def from_mate(j):
        return pltpu.make_async_remote_copy(
            xall.at[mate, j], xall.at[mate, j], psend.at[j], mrecv.at[j],
            device_id=(f, mate), device_id_type=MESH)

    def onward(block, j):
        return pltpu.make_async_remote_copy(
            part(block, j, core), part(block, j, core), fsend.at[block, j], hrecv.at[block, j, core],
            device_id=(f, mate), device_id_type=MESH)

    def arrival(block, j, which):
        return pltpu.make_async_remote_copy(
            part(block, j, which), part(block, j, which), fsend.at[block, j],
            hrecv.at[block, j, which], device_id=(f, mate), device_id_type=MESH)

    for j in range(parts):
        for copy in loads[j]:
            copy.wait()
        to_mate(j).start()

    def spread(j):
        for e in range(2):
            @pl.when(core != e)
            def _():
                from_mate(j).wait_recv()

            for i in range(peers):
                to_peer(i, j, e).start()

    spread(0)
    natural.wait()
    numbers.wait()
    for copy in halo:
        copy.wait()

    tile = LAG
    last = jnp.where(f == n - 1, total - LAG, total)

    def mask_rows(t, count):
        at = pl.multiple_of(t * tile, tile)
        here = ids[pl.ds(at, tile), :]
        there = ids[pl.ds(at + LAG, tile), :]
        row = at + lax.broadcasted_iota(jnp.int32, here.shape, 0)
        mark = jnp.where((here == there) & (row < last), 1.0, 0.0)
        mark16 = mark.astype(jnp.bfloat16)
        marks[pl.ds(at, tile), :] = mark16
        for c in range(own // 128):
            lanes = slice(c * 128, (c + 1) * 128)
            wide[0, pl.ds(at, tile), lanes] = xo[pl.ds(at, tile), lanes] * mark16
            wide[1, pl.ds(at, tile), lanes] = (
                xo[pl.ds(at + LAG, tile), lanes] * mark16)
        return count + jnp.sum(mark, axis=0, keepdims=True)

    count = lax.fori_loop(0, total // tile, mask_rows, jnp.zeros((1, 128), jnp.float32))
    row_of = lax.broadcasted_iota(jnp.int32, (EXTRA, own), 0)
    for h in range(2):
        column_sums = lax.dot_general(
            marks[...], wide[h], OVER_FRAMES, preferred_element_type=jnp.float32)[0:EXTRA]
        base[h] = jnp.where(row_of == 0, column_sums, 0.0)
        for c in range(own // 128):
            lanes = slice(c * 128, (c + 1) * 128)
            base[h, :, lanes] = jnp.where(row_of[:, lanes] == 2, count, base[h, :, lanes])

    for j in range(1, parts):
        spread(j)

    def place(u):
        k = lax.div(u, 2)
        j = lax.rem(k, parts)
        near = k < 2 * parts
        later_k = jnp.maximum(k - 2 * parts, 0)
        turn = lax.div(later_k, 2)
        far = lax.rem(chip + lax.div(turn, parts) + 1, m // 2)
        far_block = 2 * far + lax.rem(later_k, 2)
        near_block = jnp.where(k < parts, b, mate)
        return (jnp.where(near, near_block, far_block),
                jnp.where(near, j, lax.rem(turn, parts)), lax.rem(u, 2))

    def pair_copy(block, j, h):
        return pltpu.make_async_remote_copy(
            tb.at[block, j, h, 1 - side], rx.at[block, j, h], xsend.at[block, j, h], xrecv.at[block, j, h],
            device_id=(flip(f), b), device_id_type=MESH)

    def group_copy(block, j, h, p):
        return pltpu.make_async_remote_copy(
            tb.at[block, j, h, side], rz.at[block, j, h, p], zsend.at[block, j, h], zrecv.at[block, j, h, p],
            device_id=(2 * across(p) + side, b), device_id_type=MESH)

    def stage(p, q, carry):
        block, j, h = place(q)

        @pl.when(lax.rem(group, 2**p) == lax.rem(block, 2**p))
        def _():
            if p == 0:
                pair_copy(block, j, h).wait_recv()
                tb[block, j, h, side] += rx[block, j, h]
            else:
                group_copy(block, j, h, p - 1).wait_recv()
                tb[block, j, h, side] += rz[block, j, h, p - 1]
            if p < levels:
                @pl.when(bit(group, p) != bit(block, p))
                def _():
                    group_copy(block, j, h, p).start()

        return carry

    def finished(p, k):
        return jnp.maximum(k - 1 - p, 0)

    def step(k, carry):
        for p in range(levels + 1):
            lax.fori_loop(finished(p, k - 1), finished(p, k), functools.partial(stage, p), 0)

        block, j, h = place(k)

        @pl.when((k >= 4 * parts) & (h == 0))
        def _():
            arrival(block, j, core).wait_recv()
            onward(block, j).start()
            arrival(block, j, 1 - core).wait_recv()

        depth = total // 4
        for q in range(4):
            rows = slice(q * depth, (q + 1) * depth)
            granule = xall[block, j, rows, :]
            terms = lax.dot_general(
                granule, wide[h, rows, :], OVER_FRAMES, preferred_element_type=jnp.float32)
            sums = lax.dot_general(
                marks[rows, :], granule, OVER_FRAMES,
                preferred_element_type=jnp.float32)[0:EXTRA]
            sums = jnp.where(lax.broadcasted_iota(jnp.int32, sums.shape, 0) == 1, sums, 0.0)
            for half in range(2):
                value = terms[half * cw:(half + 1) * cw]
                if q == 0:
                    tb[block, j, h, half, 0:cw, :] = value
                    tb[block, j, h, half, cw:cw + EXTRA, :] = base[h]
                else:
                    tb[block, j, h, half, 0:cw, :] += value
                tb[block, j, h, half, cw:cw + EXTRA, 0:gw] += sums
        pair_copy(block, j, h).start()
        return carry

    units = 2 * steps
    lax.fori_loop(0, units, step, 0)

    def drain(k, carry):
        for p in range(levels + 1):
            lax.fori_loop(jnp.minimum(finished(p, k - 1), units), jnp.minimum(finished(p, k), units),
                          functools.partial(stage, p), 0)
        return carry

    lax.fori_loop(units, units + levels + 2, drain, 0)
    for j in range(parts):
        for h in range(2):
            out_ref[j, :, h * own:(h + 1) * own] = tb[group, j, h, side]

    for j in range(parts):
        to_mate(j).wait_send()
        for i in range(peers):
            for e in range(2):
                to_peer(i, j, e).wait_send()
                onward(2 * lax.rem(chip + i + 1, m // 2) + e, j).wait_send()
        for h in range(2):
            for i in range(m):
                pair_copy(i, j, h).wait_send()
            for i in range(1, m):
                group_copy(lax.rem(group + i, m), j, h, 0).wait_send()


def shards(n, m, frames_data, traj_ids):
    total, own = frames_data.shape
    rb = own * m // n
    levels = m.bit_length() - 1
    assert n == 2 * m and own == 2 * rb and m == 2**levels
    cw = min(128, rb)
    parts = rb // cw
    ids = jnp.broadcast_to(traj_ids[:, None], (total, 128))
    piece = (cw + EXTRA, own)
    sem = pltpu.SemaphoreType.DMA
    peers = m // 2 - 1
    reduced = pl.pallas_call(
        functools.partial(kernel, n, m, cw),
        out_shape=jax.ShapeDtypeStruct((parts, cw + EXTRA, 2 * own), jnp.float32),
        in_specs=[pl.BlockSpec(memory_space=pl.ANY)] * 2,
        out_specs=pl.BlockSpec(memory_space=pltpu.VMEM),
        scratch_shapes=[
            pltpu.VMEM((m, parts, total, 2 * cw), jnp.bfloat16),
            pltpu.VMEM((total + LAG, own), jnp.bfloat16),
            pltpu.VMEM((2, total, own), jnp.bfloat16),
            pltpu.VMEM((total + LAG, 128), jnp.int32),
            pltpu.VMEM((total, 128), jnp.bfloat16),
            pltpu.VMEM((2, EXTRA, own), jnp.float32),
            pltpu.VMEM((m, parts, 2, 2, *piece), jnp.float32),
            pltpu.VMEM((m, parts, 2, *piece), jnp.float32),
            pltpu.VMEM((m, parts, 2, levels, *piece), jnp.float32),
            sem((2 * parts + 2,)),
            sem((2,)),
            sem((2,)),
            sem((peers, parts, 2)),
            sem((parts,)),
            sem((m, parts)),
            sem((parts,)),
            sem((m, parts, 2)),
            sem((m, parts, 2)),
            sem((m, parts, 2)),
            sem((m, parts, 2)),
            sem((m, parts, 2, levels)),
        ],
        compiler_params=pltpu.CompilerParams(
            collective_id=0, has_side_effects=True, vmem_limit_bytes=58 * 2**20),
        cost_estimate=pl.CostEstimate(
            flops=4 * total * own * own * m, bytes_accessed=4 * total * own, transcendentals=0),
    )(frames_data, ids)
    side = lax.axis_index("frames") % 2
    count = reduced[0, cw + 2, 0]
    terms = reduced[:, :cw].reshape(rb, 2 * own)
    column_means = reduced[0, cw] / count
    row_sums = lax.dynamic_slice_in_dim(reduced[:, cw + 1], side * cw, cw, 1).reshape(rb)
    cov = terms / count - (row_sums / count)[:, None] * column_means[None, :]
    return cov[:, :own], cov[:, own:]


def solution(mesh):
    n, m = mesh.shape["frames"], mesh.shape["blocks"]
    return jax.shard_map(
        functools.partial(shards, n, m),
        mesh=mesh,
        in_specs=(P("frames", "blocks"), P("frames")),
        out_specs=(P("frames", "blocks"), P("frames", "blocks")),
        check_vma=False,
    )
```

```python
import functools

import jax
import jax.numpy as jnp
from jax import lax
from jax.experimental import pallas as pl
from jax.experimental.pallas import tpu as pltpu
from jax.sharding import PartitionSpec as P

LAG = 64
EXTRA = 8
MESH = pl.DeviceIdType.MESH
OVER_FRAMES = (((0,), (0,)), ((), ()))


def flip(i):
    return i + 1 - 2 * lax.rem(i, 2)


def kernel(n, m, cw, x_ref, ids_ref, out_ref, xall, xo, wide, ids, marks, base, tb, rx, rz,
           load_sem, halo_send, halo_recv, hsend, psend, fsend, mrecv, hrecv, xsend, xrecv, zsend, zrecv):
    f = lax.axis_index("frames")
    b = lax.axis_index("blocks")
    total, own = x_ref.shape
    gw = 2 * cw
    rb = own // 2
    parts = rb // cw
    peers = m // 2 - 1
    steps = m * parts
    side = lax.rem(f, 2)
    group = lax.div(f, 2)
    levels = m.bit_length() - 1
    core = lax.rem(b, 2)
    chip = lax.div(b, 2)
    span = total // 2
    mate = flip(b)
    before = lax.rem(f + n - 1, n)
    after = lax.rem(f + 1, n)

    def peer(i):
        return lax.rem(b + 2 * (i + 1), m)

    def bit(i, p):
        return lax.rem(lax.div(i, 2**p), 2)

    def across(p):
        return group + 2**p - 2 ** (p + 1) * bit(group, p)

    loads = []
    for j in range(parts):
        if parts == 1:
            loads.append([pltpu.make_async_copy(x_ref, xall.at[b, j], load_sem.at[2 * j])])
        else:
            loads.append([
                pltpu.make_async_copy(
                    x_ref.at[:, pl.ds(half * rb + j * cw, cw)],
                    xall.at[b, j, :, pl.ds(half * cw, cw)],
                    load_sem.at[2 * j + half],
                )
                for half in range(2)
            ])
    natural = pltpu.make_async_copy(x_ref, xo.at[pl.ds(0, total)], load_sem.at[2 * parts])
    numbers = pltpu.make_async_copy(ids_ref, ids.at[pl.ds(0, total)], load_sem.at[2 * parts + 1])
    for copies in loads:
        for copy in copies:
            copy.start()
    natural.start()
    numbers.start()

    barrier = pltpu.get_barrier_semaphore()

    def greet(to_frames, to_blocks):
        pl.semaphore_signal(barrier, inc=1, device_id=(to_frames, to_blocks), device_id_type=MESH)

    greet(before, b)
    greet(after, b)
    greet(flip(f), b)
    greet(f, mate)
    for i in range(peers):
        greet(f, peer(i))
    for p in range(levels):
        greet(2 * across(p) + side, b)
    pl.semaphore_wait(barrier, 4 + peers + levels)

    halo = [
        pltpu.make_async_remote_copy(
            x_ref.at[pl.ds(0, LAG)], xo.at[pl.ds(total, LAG)], halo_send.at[0], halo_recv.at[0],
            device_id=(before, b), device_id_type=MESH),
        pltpu.make_async_remote_copy(
            ids_ref.at[pl.ds(0, LAG)], ids.at[pl.ds(total, LAG)], halo_send.at[1], halo_recv.at[1],
            device_id=(before, b), device_id_type=MESH),
    ]
    for copy in halo:
        copy.start()

    def part(block, j, which):
        return xall.at[block, j, pl.ds(pl.multiple_of(which * span, 16), span)]

    def to_peer(i, j, e):
        block = 2 * chip + e
        return pltpu.make_async_remote_copy(
            part(block, j, core), part(block, j, core), hsend.at[i, j, e], hrecv.at[block, j, core],
            device_id=(f, peer(i)), device_id_type=MESH)

    def to_mate(j):
        return pltpu.make_async_remote_copy(
            xall.at[b, j], xall.at[b, j], psend.at[j], mrecv.at[j],
            device_id=(f, mate), device_id_type=MESH)

    def from_mate(j):
        return pltpu.make_async_remote_copy(
            xall.at[mate, j], xall.at[mate, j], psend.at[j], mrecv.at[j],
            device_id=(f, mate), device_id_type=MESH)

    def onward(block, j):
        return pltpu.make_async_remote_copy(
            part(block, j, core), part(block, j, core), fsend.at[block, j], hrecv.at[block, j, core],
            device_id=(f, mate), device_id_type=MESH)

    def arrival(block, j, which):
        return pltpu.make_async_remote_copy(
            part(block, j, which), part(block, j, which), fsend.at[block, j],
            hrecv.at[block, j, which], device_id=(f, mate), device_id_type=MESH)

    for j in range(parts):
        for copy in loads[j]:
            copy.wait()
        to_mate(j).start()

    def spread(j):
        for e in range(2):
            @pl.when(core != e)
            def _():
                from_mate(j).wait_recv()

            for i in range(peers):
                to_peer(i, j, e).start()

    spread(0)
    natural.wait()
    numbers.wait()
    for copy in halo:
        copy.wait()

    tile = LAG
    last = jnp.where(f == n - 1, total - LAG, total)

    def mask_rows(t, count):
        at = pl.multiple_of(t * tile, tile)
        here = ids[pl.ds(at, tile), :]
        there = ids[pl.ds(at + LAG, tile), :]
        row = at + lax.broadcasted_iota(jnp.int32, here.shape, 0)
        mark = jnp.where((here == there) & (row < last), 1.0, 0.0)
        mark16 = mark.astype(jnp.bfloat16)
        marks[pl.ds(at, tile), :] = mark16
        for c in range(own // 128):
            lanes = slice(c * 128, (c + 1) * 128)
            wide[0, pl.ds(at, tile), lanes] = xo[pl.ds(at, tile), lanes] * mark16
            wide[1, pl.ds(at, tile), lanes] = (
                xo[pl.ds(at + LAG, tile), lanes] * mark16)
        return count + jnp.sum(mark, axis=0, keepdims=True)

    count = lax.fori_loop(0, total // tile, mask_rows, jnp.zeros((1, 128), jnp.float32))
    row_of = lax.broadcasted_iota(jnp.int32, (EXTRA, own), 0)
    for h in range(2):
        column_sums = lax.dot_general(
            marks[...], wide[h], OVER_FRAMES, preferred_element_type=jnp.float32)[0:EXTRA]
        base[h] = jnp.where(row_of == 0, column_sums, 0.0)
        for c in range(own // 128):
            lanes = slice(c * 128, (c + 1) * 128)
            base[h, :, lanes] = jnp.where(row_of[:, lanes] == 2, count, base[h, :, lanes])

    for j in range(1, parts):
        spread(j)

    def place(u):
        k = lax.div(u, 2)
        j = lax.rem(k, parts)
        near = k < 2 * parts
        later_k = jnp.maximum(k - 2 * parts, 0)
        turn = lax.div(later_k, 2)
        far = lax.rem(chip + lax.div(turn, parts) + 1, m // 2)
        far_block = 2 * far + lax.rem(later_k, 2)
        near_block = jnp.where(k < parts, b, mate)
        return (jnp.where(near, near_block, far_block),
                jnp.where(near, j, lax.rem(turn, parts)), lax.rem(u, 2))

    def pair_copy(block, j, h):
        return pltpu.make_async_remote_copy(
            tb.at[block, j, h, 1 - side], rx.at[block, j, h], xsend.at[block, j, h], xrecv.at[block, j, h],
            device_id=(flip(f), b), device_id_type=MESH)

    def group_copy(block, j, h, p):
        return pltpu.make_async_remote_copy(
            tb.at[block, j, h, side], rz.at[block, j, h, p], zsend.at[block, j, h], zrecv.at[block, j, h, p],
            device_id=(2 * across(p) + side, b), device_id_type=MESH)

    def stage(p, q, carry):
        block, j, h = place(q)

        @pl.when(lax.rem(group, 2**p) == lax.rem(block, 2**p))
        def _():
            if p == 0:
                pair_copy(block, j, h).wait_recv()
                tb[block, j, h, side] += rx[block, j, h]
            else:
                group_copy(block, j, h, p - 1).wait_recv()
                tb[block, j, h, side] += rz[block, j, h, p - 1]
            if p < levels:
                @pl.when(bit(group, p) != bit(block, p))
                def _():
                    group_copy(block, j, h, p).start()

        return carry

    def finished(p, k):
        return jnp.maximum(k - 1 - 2 * p, 0)

    def step(k, carry):
        for p in range(levels + 1):
            lax.fori_loop(finished(p, k - 1), finished(p, k), functools.partial(stage, p), 0)

        block, j, h = place(k)

        @pl.when((k >= 4 * parts) & (h == 0))
        def _():
            arrival(block, j, core).wait_recv()
            onward(block, j).start()
            arrival(block, j, 1 - core).wait_recv()

        depth = total // 4
        for q in range(4):
            rows = slice(q * depth, (q + 1) * depth)
            granule = xall[block, j, rows, :]
            terms = lax.dot_general(
                granule, wide[h, rows, :], OVER_FRAMES, preferred_element_type=jnp.float32)
            sums = lax.dot_general(
                marks[rows, :], granule, OVER_FRAMES,
                preferred_element_type=jnp.float32)[0:EXTRA]
            sums = jnp.where(lax.broadcasted_iota(jnp.int32, sums.shape, 0) == 1, sums, 0.0)
            for half in range(2):
                value = terms[half * cw:(half + 1) * cw]
                if q == 0:
                    tb[block, j, h, half, 0:cw, :] = value
                    tb[block, j, h, half, cw:cw + EXTRA, :] = base[h]
                else:
                    tb[block, j, h, half, 0:cw, :] += value
                tb[block, j, h, half, cw:cw + EXTRA, 0:gw] += sums
        pair_copy(block, j, h).start()
        return carry

    units = 2 * steps
    lax.fori_loop(0, units, step, 0)

    def drain(k, carry):
        for p in range(levels + 1):
            lax.fori_loop(jnp.minimum(finished(p, k - 1), units), jnp.minimum(finished(p, k), units),
                          functools.partial(stage, p), 0)
        return carry

    lax.fori_loop(units, units + 2 * levels + 2, drain, 0)
    for j in range(parts):
        for h in range(2):
            out_ref[j, :, h * own:(h + 1) * own] = tb[group, j, h, side]

    for j in range(parts):
        to_mate(j).wait_send()
        for i in range(peers):
            for e in range(2):
                to_peer(i, j, e).wait_send()
                onward(2 * lax.rem(chip + i + 1, m // 2) + e, j).wait_send()
        for h in range(2):
            for i in range(m):
                pair_copy(i, j, h).wait_send()
            for i in range(1, m):
                group_copy(lax.rem(group + i, m), j, h, 0).wait_send()


def shards(n, m, frames_data, traj_ids):
    total, own = frames_data.shape
    rb = own * m // n
    levels = m.bit_length() - 1
    assert n == 2 * m and own == 2 * rb and m == 2**levels
    cw = min(128, rb)
    parts = rb // cw
    ids = jnp.broadcast_to(traj_ids[:, None], (total, 128))
    piece = (cw + EXTRA, own)
    sem = pltpu.SemaphoreType.DMA
    peers = m // 2 - 1
    reduced = pl.pallas_call(
        functools.partial(kernel, n, m, cw),
        out_shape=jax.ShapeDtypeStruct((parts, cw + EXTRA, 2 * own), jnp.float32),
        in_specs=[pl.BlockSpec(memory_space=pl.ANY)] * 2,
        out_specs=pl.BlockSpec(memory_space=pltpu.VMEM),
        scratch_shapes=[
            pltpu.VMEM((m, parts, total, 2 * cw), jnp.bfloat16),
            pltpu.VMEM((total + LAG, own), jnp.bfloat16),
            pltpu.VMEM((2, total, own), jnp.bfloat16),
            pltpu.VMEM((total + LAG, 128), jnp.int32),
            pltpu.VMEM((total, 128), jnp.bfloat16),
            pltpu.VMEM((2, EXTRA, own), jnp.float32),
            pltpu.VMEM((m, parts, 2, 2, *piece), jnp.float32),
            pltpu.VMEM((m, parts, 2, *piece), jnp.float32),
            pltpu.VMEM((m, parts, 2, levels, *piece), jnp.float32),
            sem((2 * parts + 2,)),
            sem((2,)),
            sem((2,)),
            sem((peers, parts, 2)),
            sem((parts,)),
            sem((m, parts)),
            sem((parts,)),
            sem((m, parts, 2)),
            sem((m, parts, 2)),
            sem((m, parts, 2)),
            sem((m, parts, 2)),
            sem((m, parts, 2, levels)),
        ],
        compiler_params=pltpu.CompilerParams(
            collective_id=0, has_side_effects=True, vmem_limit_bytes=58 * 2**20),
        cost_estimate=pl.CostEstimate(
            flops=4 * total * own * own * m, bytes_accessed=4 * total * own, transcendentals=0),
    )(frames_data, ids)
    side = lax.axis_index("frames") % 2
    count = reduced[0, cw + 2, 0]
    terms = reduced[:, :cw].reshape(rb, 2 * own)
    column_means = reduced[0, cw] / count
    row_sums = lax.dynamic_slice_in_dim(reduced[:, cw + 1], side * cw, cw, 1).reshape(rb)
    cov = terms / count - (row_sums / count)[:, None] * column_means[None, :]
    return cov[:, :own], cov[:, own:]


def solution(mesh):
    n, m = mesh.shape["frames"], mesh.shape["blocks"]
    return jax.shard_map(
        functools.partial(shards, n, m),
        mesh=mesh,
        in_specs=(P("frames", "blocks"), P("frames")),
        out_specs=(P("frames", "blocks"), P("frames", "blocks")),
        check_vma=False,
    )
```
